32 devices in a mesh: expert: 16 (over z, y, core), dp: 2 (over x).
Axes of the slice: x: 2, y: 2, z: 4, core: 2. Of those that a mesh axis runs over, the one named last changes fastest.
Arguments:
- activations: bfloat16 [512, 7168], P(('expert', 'dp')), may hold values from -6 to 6
- cotangent: bfloat16 [512, 7168], P(('expert', 'dp')), may hold values from -6 to 6
- route_ids: int32 [512, 8], P(('expert', 'dp')), may hold values from 0 to 15, all different within a row; in each aligned block of 16 rows (0 to 15, 16 to 31, ...) at most 10 rows name the same one
- route_weights: float32 [512, 8], P(('expert', 'dp')), may hold values from 0.05 to 0.6
- gate_weights: bfloat16 [16, 7168, 1024], P('expert', 'dp'), may hold values from -0.0625 to 0.0625
- up_weights: bfloat16 [16, 7168, 1024], P('expert', 'dp'), may hold values from -0.0625 to 0.0625
- down_weights: bfloat16 [16, 1024, 7168], P('expert', None, 'dp'), may hold values from -0.1875 to 0.1875
Outputs:
- grad_input: bfloat16 [512, 7168], P(('expert', 'dp'))
- grad_gate: bfloat16 [16, 7168, 1024], P('expert', 'dp')
- grad_up: bfloat16 [16, 7168, 1024], P('expert', 'dp')
- grad_down: bfloat16 [16, 1024, 7168], P('expert', None, 'dp')
The draws below stay inside these ranges and needn't reach their ends.
Inputs may be any that keep to these rules, and one draw needn't show every extreme that they name: `route_ids`: each token names 8 different experts. Among the routes of one device's 16 tokens, no expert is named more than 10 times, a bound that some block reaches.
All inputs are finite; a program needn't handle non-finite values.
Results may differ from the reference program's by a relative error of at most 0.0064.
Values may be sent and summed in bfloat16 or wider, within the bound.
A program may use at most 128 MiB of HBM per device.

```python
import math
import jax
import jax.numpy as jnp
import numpy as np
from jax import lax

D = 7168
H = 1024
TOPK = 8
TOK_DEV = 16
EXPERTS = 16
CAP = 10
TOKENS = 512


def steps_of(key, dims, shards, least, high):
    gain = 1.0
    for dim, parts in shards:
        steps = jax.random.uniform(jax.random.fold_in(jax.random.fold_in(key, 6), dim), (parts,), jnp.float32, least / len(shards), high / len(shards))
        gain = gain * jnp.repeat(jnp.exp(steps), dims[dim] // parts).reshape((-1,) + (1,) * (len(dims) - 1 - dim))
    return gain


def shared_out(rng, own, number, rows, count, top, limit, skew):
    order = jax.random.permutation(rng, count)
    crowded, ordinary = load_shares(count, rows * top, limit, skew, True), load_shares(count, rows * top, limit, skew, False)
    places = jnp.arange(count)

    def named(lengths, rotation):
        used = int((lengths > 0).sum())
        fixed = max(1, used // 4)
        passed = fixed + (places - fixed + rotation * (used - fixed)) % max(1, count - fixed)
        return jnp.zeros((count,), jnp.int32).at[order[jnp.where(places < fixed, places, passed)]].set(jnp.asarray(lengths, jnp.int32))

    lengths = jnp.where(number % 4 == 0, named(crowded, number // 4), named(ordinary, number - number // 4 - 1))
    mixed = jax.random.permutation(jax.random.fold_in(own, 3), count)
    donor, receiver = mixed[0:count // 2 * 2:2], mixed[1:count // 2 * 2:2]
    slack = jnp.minimum(lengths[donor] - 1, limit - lengths[receiver]) // 2
    slack = jnp.where((donor == order[0]) | (receiver == order[0]) | (lengths[receiver] == 0), 0, jnp.maximum(slack, 0))
    passed = jax.random.randint(jax.random.fold_in(own, 4), (count // 2,), 0, 1 << 20) % (slack + 1)
    lengths = lengths.at[donor].add(-passed).at[receiver].add(passed)
    members = jnp.searchsorted(jnp.cumsum(lengths), jnp.arange(rows * top), side="right").astype(jnp.int32)
    listing = members.reshape(top, rows).T
    listing = listing[jax.random.permutation(jax.random.fold_in(own, 1), rows)]
    rotation = jax.random.randint(jax.random.fold_in(own, 2), (rows, 1), 0, top)
    return jnp.take_along_axis(listing, (jnp.arange(top)[None, :] + rotation) % top, axis=1)


def load_shares(count, total, limit, slope, full):
    weights = [(1 << 20) // math.isqrt(rank ** slope) + 1 for rank in range(1, count + 1)]
    largest = limit if full else min(limit, max(-(-total // count), total * weights[0] // sum(weights)))
    least = 1 if total - largest >= count - 1 else 0
    counts, surplus = [largest] + [least] * (count - 1), total - largest - least * (count - 1)
    while surplus > 0:
        movable = [i for i in range(1, count) if counts[i] < largest] or [i for i in range(1, count) if counts[i] < limit]
        pool, remaining = sum([weights[i] for i in movable]), surplus
        for i in movable:
            addition = min(limit - counts[i], max(1, remaining * weights[i] // pool), surplus)
            counts[i] = counts[i] + addition
            surplus = surplus - addition
    return np.array(counts)


def normal_values(stream_key, extent, width, limit, cuts=(), held_as=jnp.bfloat16):
    values = jax.random.normal(stream_key, extent, jnp.float32) * width
    if len(cuts) > 0:
        values = steps_of(stream_key, extent, cuts, -0.22, 0.18) * values
    return jnp.clip(values, min=-limit, max=limit).astype(held_as)


def setup_inputs(seed: int = 0) -> dict:
    streams_of = jax.random.split(jax.random.key(seed), 8)
    activations = normal_values(streams_of[0], (TOKENS, D), 1.0, 6.0, ((0, 32),))
    cotangent = normal_values(streams_of[1], (TOKENS, D), 1.0, 6.0, ((0, 32),))
    route_ids_keys = jax.random.split(jax.random.fold_in(streams_of[2], 1), TOKENS // TOK_DEV)
    route_ids_turns = jax.random.permutation(jax.random.fold_in(streams_of[2], 3), TOKENS // TOK_DEV)
    route_ids = jax.vmap(lambda own, number: shared_out(jax.random.fold_in(streams_of[2], 2), own, number, TOK_DEV, EXPERTS, TOPK, CAP, 2))(route_ids_keys, route_ids_turns).reshape((TOKENS, TOPK))
    route_weights = jnp.clip(0.05 + 0.55 * jax.random.uniform(streams_of[3], (TOKENS, TOPK), jnp.float32) ** steps_of(streams_of[3], (TOKENS, TOPK), ((0, 32),), -0.2, 0.2), 0.05, 0.6)
    gate_weights = normal_values(streams_of[4], (EXPERTS, D, H), D ** -0.5, 0.0625, ((0, 16), (1, 2)))
    up_weights = normal_values(streams_of[5], (EXPERTS, D, H), D ** -0.5, 0.0625, ((0, 16), (1, 2)))
    down_weights = normal_values(streams_of[6], (EXPERTS, H, D), H ** -0.5, 0.1875, ((0, 16), (2, 2)))
    return {"activations": activations, "cotangent": cotangent, "route_ids": route_ids, "route_weights": route_weights, "gate_weights": gate_weights, "up_weights": up_weights, "down_weights": down_weights}


def swiglu_back(gate, upper, upstream):
    sigma = jax.nn.sigmoid(gate)
    silu_gate = gate * sigma
    activated = (silu_gate * upper).astype(jnp.bfloat16)
    grad_pre = (upstream * upper * sigma * (1.0 + gate * (1.0 - sigma))).astype(jnp.bfloat16)
    grad_lin = (upstream * silu_gate).astype(jnp.bfloat16)
    return grad_pre, grad_lin, activated


def reference(activations, cotangent, route_ids, route_weights, gate_weights, up_weights, down_weights):
    tokens = activations.shape[0]
    blocks = tokens // TOK_DEV
    block_ids = route_ids.reshape(blocks, TOK_DEV * TOPK)
    onehot = (block_ids[:, :, None] == jnp.arange(EXPERTS, dtype=jnp.int32)[None, None, :]).astype(jnp.int32)
    before = jnp.cumsum(onehot, axis=1) - onehot
    slot = jnp.sum(before * onehot, axis=2).astype(jnp.int32)
    row_index = (jnp.arange(blocks, dtype=jnp.int32)[:, None] * CAP + slot).reshape(-1).astype(jnp.int32)
    flat_ids = route_ids.reshape(-1).astype(jnp.int32)
    token_of = (jnp.arange(tokens * TOPK, dtype=jnp.int32) // TOPK).astype(jnp.int32)
    source = jnp.full((EXPERTS, blocks * CAP), tokens, jnp.int32).at[flat_ids, row_index].set(token_of)
    weight = jnp.zeros((EXPERTS, blocks * CAP), jnp.float32).at[flat_ids, row_index].set(route_weights.reshape(-1))
    act_pad = jnp.concatenate([activations, jnp.zeros((1, D), activations.dtype)], axis=0)
    cot_pad = jnp.concatenate([cotangent, jnp.zeros((1, D), cotangent.dtype)], axis=0)

    def one_expert(grad_rows, inputs):
        src, wgt, gate_w, up_w, down_w = inputs
        expert_input = act_pad[src]
        expert_cot = (cot_pad[src].astype(jnp.float32) * wgt[:, None]).astype(jnp.bfloat16)
        gate = jnp.dot(expert_input, gate_w, preferred_element_type=jnp.float32)
        upper = jnp.dot(expert_input, up_w, preferred_element_type=jnp.float32)
        upstream = jnp.dot(expert_cot, down_w.T, preferred_element_type=jnp.float32)
        grad_pre, grad_lin, activated = swiglu_back(gate, upper, upstream)
        g_gate = jnp.dot(expert_input.T, grad_pre, preferred_element_type=jnp.float32).astype(jnp.bfloat16)
        g_up = jnp.dot(expert_input.T, grad_lin, preferred_element_type=jnp.float32).astype(jnp.bfloat16)
        g_down = jnp.dot(activated.T, expert_cot, preferred_element_type=jnp.float32).astype(jnp.bfloat16)
        contribution = (jnp.dot(grad_pre, gate_w.T, preferred_element_type=jnp.float32)
                        + jnp.dot(grad_lin, up_w.T, preferred_element_type=jnp.float32)).astype(jnp.bfloat16)
        grad_rows = grad_rows.at[src].add(contribution.astype(jnp.float32))
        return grad_rows, (g_gate, g_up, g_down)

    start_rows = jnp.zeros((tokens + 1, D), jnp.float32)
    grad_rows, grads = lax.scan(one_expert, start_rows, (source, weight, gate_weights, up_weights, down_weights))
    grad_input = grad_rows[:tokens].astype(jnp.bfloat16)
    return grad_input, grads[0], grads[1], grads[2]
```

```python
import jax
import jax.numpy as jnp
from jax import lax
from jax.sharding import PartitionSpec as P


def swiglu_back(gate, upper, upstream):
    sigma = jax.nn.sigmoid(gate)
    silu_gate = gate * sigma
    activated = (silu_gate * upper).astype(jnp.bfloat16)
    grad_pre = (upstream * upper * sigma * (1.0 + gate * (1.0 - sigma))).astype(jnp.bfloat16)
    grad_lin = (upstream * silu_gate).astype(jnp.bfloat16)
    return (grad_pre, grad_lin, activated)


def contract_rows(left, right):
    return lax.dot_general(
        left, right, (((0,), (0,)), ((), ())), preferred_element_type=jnp.float32
    )


def contract_last(left, right):
    return lax.dot_general(
        left, right, (((1,), (1,)), ((), ())), preferred_element_type=jnp.float32
    )


def to_slices(block, num_dp):
    rows, width = block.shape
    pieces = jnp.swapaxes(block.reshape(rows, num_dp, width // num_dp), 0, 1)
    return lax.all_to_all(pieces, "dp", split_axis=0, concat_axis=0, tiled=True)


def dp_total(part, num_dp):
    sent = part.astype(jnp.bfloat16)
    total = part
    for shift in range(1, num_dp):
        got = lax.ppermute(sent, "dp", [(i, (i + shift) % num_dp) for i in range(num_dp)])
        total = total + got.astype(jnp.float32)
    return total


def placement(ids, weights, capacity, tok_rows, expert):
    tokens, topk = ids.shape
    blocks = tokens // tok_rows
    named = ids == expert
    hit = jnp.any(named, axis=1).reshape(blocks, tok_rows)
    weight = jnp.sum(jnp.where(named, weights, 0.0), axis=1)
    hit_int = hit.astype(jnp.int32)
    earlier = jnp.cumsum(hit_int, axis=1) - hit_int
    row = jnp.arange(blocks, dtype=jnp.int32)[:, None] * capacity + earlier
    row = jnp.where(hit, row, -1).reshape(tokens)
    row_iota = jnp.arange(blocks * capacity, dtype=jnp.int32)
    matches = row[None, :] == row_iota[:, None]
    row_weight = jnp.sum(jnp.where(matches, weight[None, :], 0.0), axis=1)
    return matches.astype(jnp.bfloat16), row_weight


def shards(
    activations, cotangent, route_ids, route_weights, gate_weights, up_weights, down_weights
):
    tok_rows, width = activations.shape
    topk = route_ids.shape[1]
    num_dp = lax.axis_size("dp")
    num_exp = lax.axis_size("expert")
    slice_width = gate_weights.shape[1]
    tokens = tok_rows * num_exp * num_dp
    capacity = min(tok_rows, 5 * tok_rows * topk // (4 * num_exp))
    routing = jnp.concatenate([route_ids.astype(jnp.float32), route_weights], axis=1)
    routing = lax.all_gather(routing, ("expert", "dp"), axis=0, tiled=True)
    all_act = lax.all_gather(to_slices(activations, num_dp), "expert", axis=0, tiled=True)
    all_cot = lax.all_gather(to_slices(cotangent, num_dp), "expert", axis=0, tiled=True)
    all_act = all_act.reshape(tokens, slice_width)
    all_cot = all_cot.reshape(tokens, slice_width)
    placing, row_weight = placement(
        routing[:, :topk].astype(jnp.int32),
        routing[:, topk:],
        capacity,
        tok_rows,
        lax.axis_index("expert"),
    )
    gate_local = gate_weights[0]
    up_local = up_weights[0]
    down_local = down_weights[0]
    act_rows = jnp.dot(placing, all_act, preferred_element_type=jnp.float32).astype(jnp.bfloat16)
    gate = dp_total(jnp.dot(act_rows, gate_local, preferred_element_type=jnp.float32), num_dp)
    upper = dp_total(jnp.dot(act_rows, up_local, preferred_element_type=jnp.float32), num_dp)
    cot_rows = jnp.dot(placing, all_cot, preferred_element_type=jnp.float32)
    cot_rows = (cot_rows * row_weight[:, None]).astype(jnp.bfloat16)
    upstream = dp_total(contract_last(cot_rows, down_local), num_dp)
    grad_pre, grad_lin, activated = swiglu_back(gate, upper, upstream)
    rows_back = contract_last(grad_pre, gate_local) + contract_last(grad_lin, up_local)
    rows_back = rows_back.astype(jnp.bfloat16)
    tokens_back = contract_rows(placing, rows_back).astype(jnp.bfloat16)
    arrived = lax.psum_scatter(tokens_back, "expert", scatter_dimension=0, tiled=True)
    grad_gate = contract_rows(act_rows, grad_pre).astype(jnp.bfloat16)[None]
    grad_up = contract_rows(act_rows, grad_lin).astype(jnp.bfloat16)[None]
    grad_down = contract_rows(activated, cot_rows).astype(jnp.bfloat16)[None]
    arrived = arrived.reshape(num_dp, tok_rows, slice_width)
    arrived = lax.all_to_all(arrived, "dp", split_axis=0, concat_axis=0, tiled=True)
    grad_input = jnp.swapaxes(arrived, 0, 1).reshape(tok_rows, width)
    return (grad_input, grad_gate, grad_up, grad_down)


def solution(mesh):
    placed = (
        P(("expert", "dp"), None),
        P(("expert", "dp"), None),
        P(("expert", "dp"), None),
        P(("expert", "dp"), None),
        P("expert", "dp", None),
        P("expert", "dp", None),
        P("expert", None, "dp"),
    )
    return jax.shard_map(
        shards,
        mesh=mesh,
        in_specs=placed,
        out_specs=(
            P(("expert", "dp"), None),
            P("expert", "dp", None),
            P("expert", "dp", None),
            P("expert", None, "dp"),
        ),
        check_vma=False,
    )
```

```python
import functools
import jax
import jax.numpy as jnp
from jax import lax
from jax.experimental import pallas as pl
from jax.experimental.pallas import tpu as pltpu
from jax.sharding import PartitionSpec as P


def swiglu_back(gate, upper, upstream):
    sigma = jax.nn.sigmoid(gate)
    silu_gate = gate * sigma
    activated = (silu_gate * upper).astype(jnp.bfloat16)
    grad_pre = (upstream * upper * sigma * (1.0 + gate * (1.0 - sigma))).astype(jnp.bfloat16)
    grad_lin = (upstream * silu_gate).astype(jnp.bfloat16)
    return (grad_pre, grad_lin, activated)


def contract_rows(left, right):
    return lax.dot_general(
        left, right, (((0,), (0,)), ((), ())), preferred_element_type=jnp.float32
    )


def contract_last(left, right):
    return lax.dot_general(
        left, right, (((1,), (1,)), ((), ())), preferred_element_type=jnp.float32
    )


MESH = pl.DeviceIdType.MESH
LANES = 128
CORES = 2
OUTER = 4


def gather_kernel(
    num_exp, num_dp, sent, out, own_sem, x_send, x_recv, r_send, r_recv,
    m_send, m_recv, c_send, c_recv,
):
    middle = num_exp // (OUTER * CORES)
    e = lax.axis_index("expert")
    d = lax.axis_index("dp")
    core = lax.rem(e, CORES)
    mid = lax.rem(e // CORES, middle)
    outer = e // (CORES * middle)

    def at(o, m, c):
        return (lax.rem(o + OUTER, OUTER) * middle + lax.rem(m + middle, middle)) * CORES + c

    def copy(src, dst, send, recv, device):
        return pltpu.make_async_remote_copy(
            src_ref=src, dst_ref=dst, send_sem=send, recv_sem=recv,
            device_id=device, device_id_type=MESH,
        )

    barrier = pltpu.get_barrier_semaphore()
    partners = [(e, lax.rem(d + k, num_dp)) for k in range(1, num_dp)]
    partners += [(at(outer + 1, mid, core), d), (at(outer - 1, mid, core), d)]
    partners += [(at(outer, mid + k, core), d) for k in range(1, middle)]
    partners += [(at(outer, mid, 1 - core), d)]
    for partner in partners:
        pl.semaphore_signal(barrier, inc=1, device_id=partner, device_id_type=MESH)
    pl.semaphore_wait(barrier, len(partners))

    started = []
    for k in range(1, num_dp):
        to = lax.rem(d + k, num_dp)
        c = copy(sent.at[to], out.at[e, d], x_send.at[k], x_recv.at[k], (e, to))
        c.start()
        started.append(c)
    own = pltpu.make_async_copy(sent.at[d], out.at[e, d], own_sem)
    own.start()
    own.wait()
    for k in range(1, num_dp):
        came = lax.rem(d - k + num_dp, num_dp)
        copy(sent.at[d], out.at[e, came], x_send.at[k], x_recv.at[k], (e, came)).wait_recv()

    def to_core(unit, k, s):
        c = copy(
            out.at[unit], out.at[unit], c_send.at[k, s], c_recv.at[k, s],
            (at(outer, mid, 1 - core), d),
        )
        c.start()
        started.append(c)

    def forward_middle(s):
        for k in range(1, middle):
            unit = at(outer - s, mid - k, core)
            copy(
                out.at[unit], out.at[unit], m_send.at[k, s], m_recv.at[k, s],
                (at(outer, mid - k, core), d),
            ).wait_recv()
            to_core(unit, k, s)

    for s in range(OUTER):
        unit = at(outer - s, mid, core)
        if s > 0:
            copy(
                out.at[unit], out.at[unit], r_send.at[s - 1], r_recv.at[s - 1],
                (at(outer - 1, mid, core), d),
            ).wait_recv()
        if s < OUTER - 1:
            c = copy(
                out.at[unit], out.at[unit], r_send.at[s], r_recv.at[s],
                (at(outer + 1, mid, core), d),
            )
            c.start()
            started.append(c)
        for k in range(1, middle):
            c = copy(
                out.at[unit], out.at[unit], m_send.at[k, s], m_recv.at[k, s],
                (at(outer, mid + k, core), d),
            )
            c.start()
            started.append(c)
        to_core(unit, 0, s)
        if s > 0:
            forward_middle(s - 1)
    forward_middle(OUTER - 1)
    for s in range(OUTER):
        for k in range(middle):
            unit = at(outer - s, mid - k, 1 - core)
            copy(
                out.at[unit], out.at[unit], c_send.at[k, s], c_recv.at[k, s],
                (at(outer, mid, 1 - core), d),
            ).wait_recv()
    for c in started:
        c.wait_send()


def gather_units(sent, num_exp, num_dp):
    middle = num_exp // (OUTER * CORES)
    dma = pltpu.SemaphoreType.DMA
    return pl.pallas_call(
        functools.partial(gather_kernel, num_exp, num_dp),
        out_shape=jax.ShapeDtypeStruct((num_exp,) + sent.shape, sent.dtype),
        in_specs=[pl.BlockSpec(memory_space=pl.ANY)],
        out_specs=pl.BlockSpec(memory_space=pl.ANY),
        scratch_shapes=[
            dma(()),
            dma((num_dp,)),
            dma((num_dp,)),
            dma((OUTER,)),
            dma((OUTER,)),
            dma((middle, OUTER)),
            dma((middle, OUTER)),
            dma((middle, OUTER)),
            dma((middle, OUTER)),
        ],
        compiler_params=pltpu.CompilerParams(collective_id=0, has_side_effects=True),
    )(sent)


def units_to_send(activations, cotangent, route_ids, route_weights, num_dp):
    rows, width = activations.shape
    topk = route_ids.shape[1]
    high = lax.reduce_precision(route_weights, 8, 7)
    rest = route_weights - high
    middle = lax.reduce_precision(rest, 8, 7)
    low = rest - middle
    routing = jnp.concatenate([route_ids.astype(jnp.float32), high, middle, low], axis=1)
    routing = jnp.pad(routing, ((0, 0), (0, LANES - 4 * topk))).astype(jnp.bfloat16)
    routing = jnp.broadcast_to(routing[None, None], (num_dp, 2, rows, LANES))
    both = jnp.stack([activations, cotangent]).reshape(2, rows, num_dp, width // num_dp)
    both = jnp.transpose(both, (2, 0, 1, 3))
    return jnp.concatenate([both, routing], axis=3)


def to_owners(back, num_exp, num_dp, tok_rows):
    middle = num_exp // (OUTER * CORES)
    e = lax.axis_index("expert")
    d = lax.axis_index("dp")
    core = lax.rem(e, CORES)
    mid = lax.rem(e // CORES, middle)
    outer = e // (CORES * middle)
    cols = back.shape[1]

    def shifted(o, m, c):
        return [
            (
                i,
                ((i // (CORES * middle) + o) % OUTER * middle + (i // CORES + m) % middle) * CORES
                + (i + c) % CORES,
            )
            for i in range(num_exp)
        ]

    def pick(array, index, axis):
        return lax.dynamic_index_in_dim(array, index, axis, keepdims=False)

    units = back.reshape(OUTER, middle, CORES, num_dp * tok_rows, cols)
    total = pick(units, core, 2).astype(jnp.float32)
    got = lax.ppermute(pick(units, 1 - core, 2), "expert", shifted(0, 0, 1))
    units = (total + got.astype(jnp.float32)).astype(jnp.bfloat16)
    total = pick(units, mid, 1).astype(jnp.float32)
    for k in range(1, middle):
        got = lax.ppermute(
            pick(units, lax.rem(mid + k, middle), 1), "expert", shifted(0, k, 0)
        )
        total = total + got.astype(jnp.float32)
    units = total.astype(jnp.bfloat16)
    total = pick(units, outer, 0).astype(jnp.float32)
    for k in range(1, OUTER):
        got = lax.ppermute(pick(units, lax.rem(outer + k, OUTER), 0), "expert", shifted(k, 0, 0))
        total = total + got.astype(jnp.float32)
    total = total.astype(jnp.bfloat16).reshape(num_dp, tok_rows, cols)
    pieces = jnp.zeros_like(total)
    pieces = lax.dynamic_update_index_in_dim(pieces, pick(total, d, 0), d, 0)
    for k in range(1, num_dp):
        got = lax.ppermute(
            pick(total, lax.rem(d + k, num_dp), 0),
            "dp",
            [(i, (i + k) % num_dp) for i in range(num_dp)],
        )
        pieces = lax.dynamic_update_index_in_dim(pieces, got, lax.rem(d - k + num_dp, num_dp), 0)
    return pieces


def dp_total(part, num_dp):
    sent = part.astype(jnp.bfloat16)
    total = part
    for shift in range(1, num_dp):
        got = lax.ppermute(sent, "dp", [(i, (i + shift) % num_dp) for i in range(num_dp)])
        total = total + got.astype(jnp.float32)
    return total


def placement(ids, weights, capacity, tok_rows, expert):
    tokens, topk = ids.shape
    blocks = tokens // tok_rows
    named = ids == expert
    hit = jnp.any(named, axis=1).reshape(blocks, tok_rows)
    weight = jnp.sum(jnp.where(named, weights, 0.0), axis=1)
    hit_int = hit.astype(jnp.int32)
    earlier = jnp.cumsum(hit_int, axis=1) - hit_int
    row = jnp.arange(blocks, dtype=jnp.int32)[:, None] * capacity + earlier
    row = jnp.where(hit, row, -1).reshape(tokens)
    row_iota = jnp.arange(blocks * capacity, dtype=jnp.int32)
    matches = row[None, :] == row_iota[:, None]
    row_weight = jnp.sum(jnp.where(matches, weight[None, :], 0.0), axis=1)
    return matches.astype(jnp.bfloat16), row_weight


def shards(
    activations, cotangent, route_ids, route_weights, gate_weights, up_weights, down_weights
):
    tok_rows, width = activations.shape
    topk = route_ids.shape[1]
    num_dp = lax.axis_size("dp")
    num_exp = lax.axis_size("expert")
    slice_width = gate_weights.shape[1]
    tokens = tok_rows * num_exp * num_dp
    capacity = min(tok_rows, 5 * tok_rows * topk // (4 * num_exp))
    sent = units_to_send(activations, cotangent, route_ids, route_weights, num_dp)
    units = gather_units(sent, num_exp, num_dp)
    all_act = units[:, :, 0, :, :slice_width].reshape(tokens, slice_width)
    all_cot = units[:, :, 1, :, :slice_width].reshape(tokens, slice_width)
    routing = units[:, :, 0, :, slice_width:].astype(jnp.float32).reshape(tokens, LANES)
    weights = routing[:, topk : 2 * topk] + routing[:, 2 * topk : 3 * topk]
    placing, row_weight = placement(
        routing[:, :topk].astype(jnp.int32),
        weights + routing[:, 3 * topk : 4 * topk],
        capacity,
        tok_rows,
        lax.axis_index("expert"),
    )
    gate_local = gate_weights[0]
    up_local = up_weights[0]
    down_local = down_weights[0]
    act_rows = jnp.dot(placing, all_act, preferred_element_type=jnp.float32).astype(jnp.bfloat16)
    gate = dp_total(jnp.dot(act_rows, gate_local, preferred_element_type=jnp.float32), num_dp)
    upper = dp_total(jnp.dot(act_rows, up_local, preferred_element_type=jnp.float32), num_dp)
    cot_rows = jnp.dot(placing, all_cot, preferred_element_type=jnp.float32)
    cot_rows = (cot_rows * row_weight[:, None]).astype(jnp.bfloat16)
    upstream = dp_total(contract_last(cot_rows, down_local), num_dp)
    grad_pre, grad_lin, activated = swiglu_back(gate, upper, upstream)
    halves = []
    half = slice_width // 2
    for start in (0, half):
        rows_back = contract_last(grad_pre, gate_local[start : start + half])
        rows_back = rows_back + contract_last(grad_lin, up_local[start : start + half])
        back = contract_rows(placing, rows_back.astype(jnp.bfloat16)).astype(jnp.bfloat16)
        halves.append(to_owners(back, num_exp, num_dp, tok_rows))
    grad_gate = contract_rows(act_rows, grad_pre).astype(jnp.bfloat16)[None]
    grad_up = contract_rows(act_rows, grad_lin).astype(jnp.bfloat16)[None]
    grad_down = contract_rows(activated, cot_rows).astype(jnp.bfloat16)[None]
    arrived = jnp.concatenate(halves, axis=2)
    grad_input = jnp.swapaxes(arrived, 0, 1).reshape(tok_rows, width)
    return (grad_input, grad_gate, grad_up, grad_down)


def solution(mesh):
    placed = (
        P(("expert", "dp"), None),
        P(("expert", "dp"), None),
        P(("expert", "dp"), None),
        P(("expert", "dp"), None),
        P("expert", "dp", None),
        P("expert", "dp", None),
        P("expert", None, "dp"),
    )
    return jax.shard_map(
        shards,
        mesh=mesh,
        in_specs=placed,
        out_specs=(
            P(("expert", "dp"), None),
            P("expert", "dp", None),
            P("expert", "dp", None),
            P("expert", None, "dp"),
        ),
        check_vma=False,
    )
```
